256 devices in a mesh: row: 16 (over z, y_hi), col: 16 (over x, y_lo, core).
Axes of the slice: x: 4, y: 4 (y_hi: 2, y_lo: 2; y = y_hi * 2 + y_lo), z: 8, core: 2. Of those that a mesh axis runs over, the one named last changes fastest.
Arguments:
- amplitudes: float32 [512, 512], P(('col', 'row')), may hold values from -6 to 6
- integrals: float32 [512, 184320], P('col', 'row'), may hold values from -0.25 to 0.25
- previous: float32 [512, 184320], P('col', 'row'), may hold values from -6 to 6
Outputs:
- residual: float32 [512, 184320], P('col', 'row')
The draws below stay inside these ranges and needn't reach their ends.
All inputs are finite; a program needn't handle non-finite values.
Results may differ from the reference program's by a relative error of at most 0.000051.
Values sent between devices are 32-bit elements; how exact they have to be, the bound alone decides.
No kernel may reach another device: no remote copies, remote signals or barrier semaphores. Data moves between devices by JAX's collectives and lax.ppermute only.
A program may use at most 128 MiB of HBM per device.

```python
import jax
import jax.numpy as jnp
from jax import lax

AB = 184320
K = 512
PAIRS = 512


def levels(own_key, shape, split, low, largest):
    def one(axis_at, parts):
        steps = jax.random.uniform(jax.random.fold_in(jax.random.fold_in(own_key, 6), axis_at), (parts,), jnp.float32, low / len(split), largest / len(split))
        return jnp.repeat(jnp.exp(steps), shape[axis_at] // parts).reshape((-1,) + (1,) * (len(shape) - axis_at - 1))

    level = one(*split[0])
    for cut in split[1:]:
        level = level * one(*cut)
    return level


def scatter_about(own_key, extent, deviation, bound, shards=(), held_as=jnp.bfloat16):
    result = jax.random.normal(own_key, extent, jnp.float32) * deviation
    if len(shards) > 0:
        result = levels(own_key, extent, shards, -0.22, 0.18) * result
    return jnp.clip(result, min=-bound, max=bound).astype(held_as)


def setup_inputs(seed: int = 0) -> dict:
    key_of = jax.random.split(jax.random.key(seed), 4)
    return {
        "amplitudes": scatter_about(key_of[0], (PAIRS, K), 1.0, 6.0, ((0, 256),), jnp.float32),
        "integrals": scatter_about(key_of[1], (K, AB), K ** -0.5, 0.25, ((0, 16), (1, 16)), jnp.float32),
        "previous": scatter_about(key_of[2], (PAIRS, AB), 1.0, 6.0, ((0, 16), (1, 16)), jnp.float32),
    }


def reference(amplitudes, integrals, previous):
    ladder = jnp.dot(amplitudes, integrals, precision=lax.Precision.HIGHEST, preferred_element_type=jnp.float32)
    return previous + ladder
```

```python
import functools

import jax
import jax.numpy as jnp
from jax import lax
from jax.experimental import pallas as pl
from jax.experimental.pallas import tpu as pltpu
from jax.sharding import PartitionSpec as P

LANES = 128
ROWS = 32
TILES = 11
SPLIT = 8 * TILES * LANES
MSG = TILES * ROWS + 8
OFFSETS = [(dx, dy) for dx in range(4) for dy in range(2)]
ORDER = [1, 4, 3, 2, 7, 6, 5]
MIB = 1 << 20


def cols(f):
    pairs = []
    for c in range(16):
        x, y, k = f(c >> 2, (c >> 1) & 1, c & 1)
        pairs.append((c, 4 * (x % 4) + 2 * (y % 2) + k % 2))
    return pairs


def everywhere(f):
    pairs = []
    for d in range(256):
        r, c = d >> 4, d & 15
        x, y, z, k = f(c >> 2, 2 * (r & 1) + ((c >> 1) & 1), r >> 1, c & 1)
        x, y, z, k = x % 4, y % 4, z % 8, k % 2
        pairs.append((d, 16 * (2 * z + (y >> 1)) + 4 * x + 2 * (y & 1) + k))
    return pairs


def move(a, dx, dy):
    return lax.ppermute(a, "col", cols(lambda x, y, k: (x + dx, y + dy, k)))


def swap_cores(a):
    return lax.ppermute(a, "col", cols(lambda x, y, k: (x, y, k + 1)))


def shift(a, f):
    return lax.ppermute(a, ("row", "col"), everywhere(f))


def here():
    col, row = lax.axis_index("col"), lax.axis_index("row")
    return col // 4, (col // 2) % 2, col % 2, row


def chip(x, y, o, sign):
    dx, dy = OFFSETS[o]
    return 2 * ((x + 4 + sign * dx) % 4) + (y + dy) % 2


def split(a):
    hi = a.astype(jnp.bfloat16)
    return hi, (a - hi.astype(jnp.float32)).astype(jnp.bfloat16)


def lane_group():
    return lax.broadcasted_iota(jnp.int32, (8, LANES), 1) // ROWS


def pack_kernel(v, *msgs):
    x, y, _, _ = here()
    group = lane_group()
    for o, msg in enumerate(msgs):
        q = chip(x, y, o, 1)
        for t in range(TILES):
            at = pl.multiple_of((q * TILES + t) * LANES, LANES)
            msg[t * ROWS : (t + 1) * ROWS, :] = v[:, pl.ds(at, LANES)]
        at = pl.multiple_of(SPLIT + (q // 4) * LANES, LANES)
        folded = jnp.zeros((8, LANES), jnp.float32)
        for g in range(4):
            part = v[8 * g : 8 * g + 8, pl.ds(at, LANES)]
            part = pltpu.roll(part, (ROWS * (g + 4 - q % 4)) % LANES, 1)
            folded = jnp.where(group == g, part, folded)
        msg[TILES * ROWS :, :] = folded


def amplitudes_kernel(*refs):
    parts, (hi_out, lo_out) = refs[:4], refs[4:6]
    x, y_lo, k, row = here()
    y, z = 2 * (row % 2) + y_lo, row // 2
    s = lax.broadcasted_iota(jnp.int32, (256, 256), 1)
    d = lax.broadcasted_iota(jnp.int32, (256, 256), 0)
    i, jy, jx, j4, jz = s % 2, (s // 2) % 4, (s // 8) % 4, (s // 32) % 2, s // 64
    back = jnp.where(jz == 0, 0, jnp.where(jz == 1, 1, jnp.where(jz == 2, 7, jnp.where(k == 0, 2, 6))))
    from_x, from_y, from_z = (x + 4 - jx) % 4, (y + 4 - jy) % 4, (z + 16 - back - 4 * j4) % 8
    offset = 2 * ((from_x + 4 - x) % 4) + (from_y + y_lo) % 2
    target = offset * ROWS + 2 * (2 * from_z + from_y // 2) + i
    order = jnp.where(d == target, 1.0, 0.0).astype(jnp.bfloat16)
    for c in range(4):
        rows = jnp.concatenate([p[pl.ds(c, 64, stride=4), :] for p in parts], axis=0)
        for piece, out in zip(split(rows), (hi_out, lo_out)):
            out[:, c * LANES : (c + 1) * LANES] = jnp.dot(
                order, piece, preferred_element_type=jnp.float32
            ).astype(jnp.bfloat16)


def ladder_kernel(*refs):
    mine, other, (t_hi, t_lo) = refs[:8], refs[8:16], refs[16:18]
    msgs, (v_hi, v_lo) = refs[18:26], refs[26:28]
    x, y, k, _ = here()
    group = lane_group()
    for o in range(8):
        q = chip(x, y, o, -1)
        for core, blocks in ((k, mine), (1 - k, other)):
            at = pl.multiple_of((2 * q + core) * ROWS, ROWS)
            for t in range(TILES):
                hi, lo = split(blocks[o][t * ROWS : (t + 1) * ROWS, :])
                v_hi[pl.ds(at, ROWS), t * LANES : (t + 1) * LANES] = hi
                v_lo[pl.ds(at, ROWS), t * LANES : (t + 1) * LANES] = lo
            folded = blocks[o][TILES * ROWS :, :]
            rows = [folded] + [pltpu.roll(folded, LANES - ROWS * g, 1) for g in range(1, 4)]
            hi, lo = split(jnp.concatenate(rows, axis=0))
            v_hi[pl.ds(at, ROWS), TILES * LANES :] = hi
            v_lo[pl.ds(at, ROWS), TILES * LANES :] = lo
    dot = functools.partial(jnp.dot, preferred_element_type=jnp.float32)
    for j in range(6):
        lanes = slice(2 * j * LANES, (2 * j + 2) * LANES)
        hi, lo = v_hi[:, lanes], v_lo[:, lanes]
        out = dot(t_hi[...], hi) + (dot(t_hi[...], lo) + dot(t_lo[...], hi))
        for o in range(8):
            rows = out[o * ROWS : (o + 1) * ROWS]
            msgs[o][2 * j * ROWS : (2 * j + 1) * ROWS, :] = rows[:, :LANES]
            if j < 5:
                msgs[o][(2 * j + 1) * ROWS : (2 * j + 2) * ROWS, :] = rows[:, LANES:]
            else:
                folded = rows[:8, LANES:]
                for g in range(1, 4):
                    part = pltpu.roll(rows[8 * g : 8 * g + 8, LANES:], ROWS * g, 1)
                    folded = jnp.where(group == g, part, folded)
                msgs[o][TILES * ROWS :, :] = folded


def add_kernel(*refs):
    msgs, previous, out = refs[:8], refs[8], refs[9]
    x, y, _, _ = here()
    group = lane_group()
    narrow = [[jnp.zeros((8, LANES), jnp.float32) for _ in range(4)] for _ in range(2)]
    for o in range(8):
        q = chip(x, y, o, -1)
        for t in range(TILES):
            at = pl.ds(pl.multiple_of((q * TILES + t) * LANES, LANES), LANES)
            out[:, at] = previous[:, at] + msgs[o][t * ROWS : (t + 1) * ROWS, :]
        folded = msgs[o][TILES * ROWS :, :]
        for g in range(4):
            part = pltpu.roll(folded, (ROWS * (q % 4 + 4 - g)) % LANES, 1)
            for j in range(2):
                narrow[j][g] = jnp.where(group + 4 * j == q, part, narrow[j][g])
    for j in range(2):
        at = slice(SPLIT + j * LANES, SPLIT + (j + 1) * LANES)
        out[:, at] = previous[:, at] + jnp.concatenate(narrow[j], axis=0)


def call(kernel, outs, args, flops=0, scratch=(), limit=16):
    moved = sum(a.size * a.dtype.itemsize for a in list(args) + list(outs))
    return pl.pallas_call(
        kernel,
        out_shape=outs,
        in_specs=[pl.BlockSpec(memory_space=pltpu.VMEM)] * len(args),
        out_specs=jax.tree.map(lambda _: pl.BlockSpec(memory_space=pltpu.VMEM), outs),
        scratch_shapes=list(scratch),
        compiler_params=pltpu.CompilerParams(vmem_limit_bytes=limit * MIB),
        cost_estimate=pl.CostEstimate(flops=flops, bytes_accessed=moved, transcendentals=0),
    )(*args)


def gather_amplitudes(a):
    part = a.reshape(8, LANES)
    part = jnp.concatenate([part] + [shift(part, lambda x, y, z, k, j=j: (x, y + j, z, k)) for j in range(1, 4)], 0)
    part = jnp.concatenate([part] + [shift(part, lambda x, y, z, k, j=j: (x + j, y, z, k)) for j in range(1, 4)], 0)
    part = jnp.concatenate([part, shift(part, lambda x, y, z, k: (x, y, z + 4, k))], 0)
    return [
        part,
        shift(part, lambda x, y, z, k: (x, y, z + 1, k)),
        shift(part, lambda x, y, z, k: (x, y, z - 1, k)),
        shift(part, lambda x, y, z, k: (x, y, z + 2 - 4 * k, k)),
    ]


def body(amplitudes, integrals, previous):
    msg = jax.ShapeDtypeStruct((MSG, LANES), jnp.float32)
    t_shape = jax.ShapeDtypeStruct((256, 512), jnp.bfloat16)
    sent = call(pack_kernel, [msg] * 8, [integrals])
    mine = {0: sent[0]}
    for o in ORDER:
        mine[o] = move(sent[o], *OFFSETS[o])
    mine = [mine[o] for o in range(8)]
    other = [swap_cores(m) for m in mine]
    t_hi, t_lo = call(amplitudes_kernel, [t_shape] * 2, gather_amplitudes(amplitudes), 2 * 256 * 256 * 1024)
    sent = call(
        ladder_kernel,
        [msg] * 8,
        mine + other + [t_hi, t_lo],
        3 * 2 * 256 * 512 * 1440,
        [pltpu.VMEM((512, 12 * LANES), jnp.bfloat16)] * 2,
        24,
    )
    back = {0: sent[0]}
    for o in ORDER:
        back[o] = move(sent[o], *OFFSETS[o])
    out = jax.ShapeDtypeStruct(previous.shape, jnp.float32)
    return call(add_kernel, [out], [back[o] for o in range(8)] + [previous])[0]


def solution(mesh):
    in_specs = (P(("col", "row"), None), P("col", "row"), P("col", "row"))
    out_specs = P("col", "row")
    return jax.shard_map(body, mesh=mesh, in_specs=in_specs, out_specs=out_specs, check_vma=False)
```

```python
import functools

import jax
import jax.numpy as jnp
from jax import lax
from jax.experimental import pallas as pl
from jax.experimental.pallas import tpu as pltpu
from jax.sharding import PartitionSpec as P

LANES = 128
ROWS = 32
TILES = 11
SPLIT = 8 * TILES * LANES
MSG = TILES * ROWS + 8
MIB = 1 << 20
OVER_CHIPS = [[c for c in range(16) if c % 2 == k] for k in range(2)]
OFFSETS = [(dx, dy) for dx in range(4) for dy in range(2)]


def cols(f):
    pairs = []
    for c in range(16):
        x, y, k = f(c >> 2, (c >> 1) & 1, c & 1)
        pairs.append((c, 4 * (x % 4) + 2 * (y % 2) + k % 2))
    return pairs


def rows(f):
    pairs = []
    for d in range(256):
        r, c = d >> 4, d & 15
        z, y = f(r >> 1, r & 1, c & 1)
        pairs.append((d, 16 * (2 * (z % 8) + y % 2) + c))
    return pairs


def over_chips(a):
    return lax.all_to_all(a, "col", 0, 0, tiled=True, axis_index_groups=OVER_CHIPS)


def to_chip(a, dx, dy):
    return lax.ppermute(a, "col", cols(lambda x, y, k: (x + dx, y + dy, k)))


def swap_cores(a):
    return lax.ppermute(a, "col", cols(lambda x, y, k: (x, y, k + 1)))


def over_rows(a, f):
    return lax.ppermute(a, ("row", "col"), rows(f))


def here():
    col, row = lax.axis_index("col"), lax.axis_index("row")
    return col // 4, (col // 2) % 2, col % 2, row


def split(a):
    hi = a.astype(jnp.bfloat16)
    return hi, (a - hi.astype(jnp.float32)).astype(jnp.bfloat16)


def lane_group():
    return lax.broadcasted_iota(jnp.int32, (8, LANES), 1) // ROWS


def pack_kernel(v, msgs):
    for q in range(8):
        for t in range(TILES):
            at = (q * TILES + t) * LANES
            msgs[q, t * ROWS : (t + 1) * ROWS, :] = v[:, at : at + LANES]
        at = SPLIT + q // 4 * LANES
        folded = v[:8, at : at + LANES]
        for g in range(4):
            part = pltpu.roll(v[8 * g : 8 * g + 8, at : at + LANES], (ROWS * (g + 4 - q % 4)) % LANES, 1)
            folded = jnp.where(lane_group() == g, part, folded)
        msgs[q, TILES * ROWS :, :] = folded


def tile_kernel(a, out):
    out[...] = jnp.concatenate([a[i : i + 1, c * LANES : (c + 1) * LANES] for i in range(2) for c in range(4)], axis=0)


def join_kernel(a, b, out):
    n = a.shape[0]
    out[:n, :] = a[...]
    out[n:, :] = b[...]


def collect_kernel(*refs):
    parts, out = refs[:4], refs[4]
    _, _, k, row = here()
    for jz, part in enumerate(parts):
        back = (0, 1, 7, 2 + 4 * k)[jz]
        for j4 in range(2):
            for jy in range(2):
                r = 2 * ((row // 2 + 16 - back - 4 * j4) % 8) + (row + jy) % 2
                j = 2 * j4 + jy
                out[pl.ds(pl.multiple_of(8 * r, 8), 8), :] = part[8 * j : 8 * j + 8, :]


def unpack(msg, v_hi, v_lo, at):
    at = pl.ds(pl.multiple_of(at, ROWS), ROWS)
    for t in range(TILES):
        hi, lo = split(msg[t * ROWS : (t + 1) * ROWS, :])
        v_hi[at, t * LANES : (t + 1) * LANES] = hi
        v_lo[at, t * LANES : (t + 1) * LANES] = lo
    folded = msg[TILES * ROWS :, :]
    rows = [folded] + [pltpu.roll(folded, LANES - ROWS * g, 1) for g in range(1, 4)]
    hi, lo = split(jnp.concatenate(rows, axis=0))
    v_hi[at, TILES * LANES :] = hi
    v_lo[at, TILES * LANES :] = lo


def ladder(t_hi, t_lo, v_hi, v_lo, msgs):
    dot = functools.partial(jnp.dot, preferred_element_type=jnp.float32)
    for j in range(6):
        lanes = slice(2 * j * LANES, (2 * j + 2) * LANES)
        hi, lo = v_hi[:, lanes], v_lo[:, lanes]
        out = dot(t_hi, hi) + (dot(t_hi, lo) + dot(t_lo, hi))
        for q, msg in enumerate(msgs):
            rows = out[q * ROWS : (q + 1) * ROWS]
            msg[2 * j * ROWS : (2 * j + 1) * ROWS, :] = rows[:, :LANES]
            if j < 5:
                msg[(2 * j + 1) * ROWS : (2 * j + 2) * ROWS, :] = rows[:, LANES:]
            else:
                folded = rows[:8, LANES:]
                for g in range(1, 4):
                    part = pltpu.roll(rows[8 * g : 8 * g + 8, LANES:], ROWS * g, 1)
                    folded = jnp.where(lane_group() == g, part, folded)
                msg[TILES * ROWS :, :] = folded


def amplitude_rows(amps):
    his, los = [], []
    for amp in amps:
        parts = [split(amp[pl.ds(c, ROWS, stride=4), :]) for c in range(4)]
        his.append(jnp.concatenate([p[0] for p in parts], axis=1))
        los.append(jnp.concatenate([p[1] for p in parts], axis=1))
    return jnp.concatenate(his, axis=0), jnp.concatenate(los, axis=0)


def first_kernel(n, mine, other, *refs):
    amps, msgs, (v_hi, v_lo) = refs[:n], refs[n : 2 * n], refs[2 * n :]
    _, _, k, _ = here()
    for q in range(8):
        unpack(mine.at[q], v_hi, v_lo, (2 * q + k) * ROWS)
        unpack(other.at[q], v_hi, v_lo, (2 * q + 1 - k) * ROWS)
    ladder(*amplitude_rows(amps), v_hi, v_lo, msgs)


def later_kernel(n, v_hi, v_lo, *refs):
    ladder(*amplitude_rows(refs[:n]), v_hi, v_lo, refs[n:])


def chip(o, sign, relative):
    if not relative:
        return o
    x, y, _, _ = here()
    dx, dy = OFFSETS[o]
    return 2 * ((x + 4 + sign * dx) % 4) + (y + dy) % 2


def add_rel_kernel(*refs):
    msgs, previous, out = refs[:8], refs[8], refs[9]
    group = lane_group()
    narrow = [[jnp.zeros((8, LANES), jnp.float32) for _ in range(4)] for _ in range(2)]
    for o in range(8):
        q = chip(o, -1, True)
        for t in range(TILES):
            at = pl.ds(pl.multiple_of((q * TILES + t) * LANES, LANES), LANES)
            out[:, at] = previous[:, at] + msgs[o][t * ROWS : (t + 1) * ROWS, :]
        folded = msgs[o][TILES * ROWS :, :]
        for g in range(4):
            part = pltpu.roll(folded, (ROWS * (q % 4 + 4 - g)) % LANES, 1)
            for j in range(2):
                narrow[j][g] = jnp.where(group + 4 * j == q, part, narrow[j][g])
    for j in range(2):
        at = slice(SPLIT + j * LANES, SPLIT + (j + 1) * LANES)
        out[:, at] = previous[:, at] + jnp.concatenate(narrow[j], axis=0)


def call(kernel, outs, args, flops=0, scratch=(), limit=16):
    moved = sum(a.size * a.dtype.itemsize for a in list(args) + list(outs))
    return pl.pallas_call(
        kernel,
        out_shape=outs,
        in_specs=[pl.BlockSpec(memory_space=pltpu.VMEM)] * len(args),
        out_specs=jax.tree.map(lambda _: pl.BlockSpec(memory_space=pltpu.VMEM), outs),
        scratch_shapes=list(scratch),
        compiler_params=pltpu.CompilerParams(vmem_limit_bytes=limit * MIB),
        cost_estimate=pl.CostEstimate(flops=flops, bytes_accessed=moved, transcendentals=0),
    )(*args)


def f32(*shape):
    return jax.ShapeDtypeStruct(shape, jnp.float32)


GROUPS = [[(0, 0), (0, 1)], [(1, 0), (1, 1), (3, 0), (3, 1)], [(2, 0), (2, 1)]]


def body(amplitudes, integrals, previous):
    msg, stack = f32(MSG, LANES), f32(8, MSG, LANES)
    tile = call(tile_kernel, [f32(8, LANES)], [amplitudes])[0]
    part = call(join_kernel, [f32(16, LANES)], [tile, over_rows(tile, lambda z, y, k: (z, y + 1))])[0]
    sent = call(pack_kernel, [stack], [integrals])[0]
    sent, part = lax.optimization_barrier((sent, part))
    part = call(join_kernel, [f32(32, LANES)], [part, over_rows(part, lambda z, y, k: (z + 4, y))])[0]
    parts = [
        part,
        over_rows(part, lambda z, y, k: (z + 1, y)),
        over_rows(part, lambda z, y, k: (z - 1, y)),
        over_rows(part, lambda z, y, k: (z + 2 - 4 * k, y)),
    ]
    own = call(collect_kernel, [f32(128, LANES)], parts)[0]
    mine, _ = lax.optimization_barrier((over_chips(sent), own))
    amps = {o: to_chip(own, *o) for o in [(0, 1), (1, 0), (3, 0), (1, 1), (3, 1), (2, 0), (2, 1)]}
    amps[(0, 0)] = own
    other = swap_cores(mine)
    flops = 3 * 2 * 32 * 512 * 1440
    v_shape = jax.ShapeDtypeStruct((512, 12 * LANES), jnp.bfloat16)
    back = {}
    for i, group in enumerate(GROUPS):
        n = len(group)
        rows = [amps[o] for o in group]
        if i == 0:
            kernel, outs, args = first_kernel, [msg] * n + [v_shape] * 2, [mine, other] + rows
        else:
            if i == 2:
                *v, back[(0, 1)] = lax.optimization_barrier((*v, back[(0, 1)]))
            kernel, outs, args = later_kernel, [msg] * n, v + rows
        out = call(functools.partial(kernel, n), outs, args, n * flops, limit=32)
        v = list(out[n:]) if i == 0 else v
        for (dx, dy), m in zip(group, out):
            o = ((4 - dx) % 4, dy)
            back[o] = m if o == (0, 0) else to_chip(m, *o)
    return call(add_rel_kernel, [f32(*previous.shape)], [back[o] for o in OFFSETS] + [previous])[0]


def solution(mesh):
    in_specs = (P(("col", "row"), None), P("col", "row"), P("col", "row"))
    out_specs = P("col", "row")
    return jax.shard_map(body, mesh=mesh, in_specs=in_specs, out_specs=out_specs, check_vma=False)
```

```python
import functools

import jax
import jax.numpy as jnp
from jax import lax
from jax.experimental import pallas as pl
from jax.experimental.pallas import tpu as pltpu
from jax.sharding import PartitionSpec as P

LANES = 128
ROWS = 32
TILES = 11
SPLIT = 8 * TILES * LANES
MSG = TILES * ROWS + 8
MIB = 1 << 20
OVER_CHIPS = [[c for c in range(16) if c % 2 == k] for k in range(2)]
OFFSETS = [(dx, dy) for dx in range(4) for dy in range(2)]


def cols(f):
    pairs = []
    for c in range(16):
        x, y, k = f(c >> 2, (c >> 1) & 1, c & 1)
        pairs.append((c, 4 * (x % 4) + 2 * (y % 2) + k % 2))
    return pairs


def rows(f):
    pairs = []
    for d in range(256):
        r, c = d >> 4, d & 15
        z, y = f(r >> 1, r & 1, c & 1)
        pairs.append((d, 16 * (2 * (z % 8) + y % 2) + c))
    return pairs


def over_chips(a):
    return lax.all_to_all(a, "col", 0, 0, tiled=True, axis_index_groups=OVER_CHIPS)


def to_chip(a, dx, dy):
    return lax.ppermute(a, "col", cols(lambda x, y, k: (x + dx, y + dy, k)))


def swap_cores(a):
    return lax.ppermute(a, "col", cols(lambda x, y, k: (x, y, k + 1)))


def over_rows(a, f):
    return lax.ppermute(a, ("row", "col"), rows(f))


def here():
    col, row = lax.axis_index("col"), lax.axis_index("row")
    return col // 4, (col // 2) % 2, col % 2, row


def split(a):
    hi = a.astype(jnp.bfloat16)
    return hi, (a - hi.astype(jnp.float32)).astype(jnp.bfloat16)


def lane_group():
    return lax.broadcasted_iota(jnp.int32, (8, LANES), 1) // ROWS


def pack_kernel(v, msgs):
    for q in range(8):
        for t in range(TILES):
            at = (q * TILES + t) * LANES
            msgs[q, t * ROWS : (t + 1) * ROWS, :] = v[:, at : at + LANES]
        at = SPLIT + q // 4 * LANES
        folded = v[:8, at : at + LANES]
        for g in range(4):
            part = pltpu.roll(v[8 * g : 8 * g + 8, at : at + LANES], (ROWS * (g + 4 - q % 4)) % LANES, 1)
            folded = jnp.where(lane_group() == g, part, folded)
        msgs[q, TILES * ROWS :, :] = folded


def tiles_kernel(a, b, out):
    for n, part in enumerate((a, b)):
        rows = [part[i : i + 1, c * LANES : (c + 1) * LANES] for i in range(2) for c in range(4)]
        out[8 * n : 8 * n + 8, :] = jnp.concatenate(rows, axis=0)


def join_kernel(a, b, out):
    n = a.shape[0]
    out[:n, :] = a[...]
    out[n:, :] = b[...]


def collect_kernel(*refs):
    parts, out = refs[:4], refs[4]
    _, _, k, row = here()
    for jz, part in enumerate(parts):
        back = (0, 1, 7, 2 + 4 * k)[jz]
        for j4 in range(2):
            for jy in range(2):
                r = 2 * ((row // 2 + 16 - back - 4 * j4) % 8) + (row + jy) % 2
                j = 2 * j4 + jy
                out[pl.ds(pl.multiple_of(8 * r, 8), 8), :] = part[8 * j : 8 * j + 8, :]


def unpack(msg, v_hi, v_lo, at):
    at = pl.ds(pl.multiple_of(at, ROWS), ROWS)
    for t in range(TILES):
        hi, lo = split(msg[t * ROWS : (t + 1) * ROWS, :])
        v_hi[at, t * LANES : (t + 1) * LANES] = hi
        v_lo[at, t * LANES : (t + 1) * LANES] = lo
    folded = msg[TILES * ROWS :, :]
    rows = [folded] + [pltpu.roll(folded, LANES - ROWS * g, 1) for g in range(1, 4)]
    hi, lo = split(jnp.concatenate(rows, axis=0))
    v_hi[at, TILES * LANES :] = hi
    v_lo[at, TILES * LANES :] = lo


def ladder(t_hi, t_lo, v_hi, v_lo, msgs):
    dot = functools.partial(jnp.dot, preferred_element_type=jnp.float32)
    for j in range(6):
        lanes = slice(2 * j * LANES, (2 * j + 2) * LANES)
        hi, lo = v_hi[:, lanes], v_lo[:, lanes]
        out = dot(t_hi, hi) + (dot(t_hi, lo) + dot(t_lo, hi))
        for q, msg in enumerate(msgs):
            rows = out[q * ROWS : (q + 1) * ROWS]
            msg[2 * j * ROWS : (2 * j + 1) * ROWS, :] = rows[:, :LANES]
            if j < 5:
                msg[(2 * j + 1) * ROWS : (2 * j + 2) * ROWS, :] = rows[:, LANES:]
            else:
                folded = rows[:8, LANES:]
                for g in range(1, 4):
                    part = pltpu.roll(rows[8 * g : 8 * g + 8, LANES:], ROWS * g, 1)
                    folded = jnp.where(lane_group() == g, part, folded)
                msg[TILES * ROWS :, :] = folded


def amplitude_rows(amps):
    his, los = [], []
    for amp in amps:
        for h in range(2):
            parts = [split(amp[pl.ds(128 * h + c, ROWS, stride=4), :]) for c in range(4)]
            his.append(jnp.concatenate([p[0] for p in parts], axis=1))
            los.append(jnp.concatenate([p[1] for p in parts], axis=1))
    return jnp.concatenate(his, axis=0), jnp.concatenate(los, axis=0)


def first_kernel(mine, other, amp, *refs):
    msgs, (v_hi, v_lo) = refs[:2], refs[2:4]
    _, _, k, _ = here()
    for q in range(8):
        unpack(mine.at[q], v_hi, v_lo, (2 * q + k) * ROWS)
        unpack(other.at[q], v_hi, v_lo, (2 * q + 1 - k) * ROWS)
    t_hi, t_lo = amplitude_rows([amp])
    ladder(t_hi, t_lo, v_hi, v_lo, msgs)


def later_kernel(n, v_hi, v_lo, *refs):
    t_hi, t_lo = amplitude_rows(refs[:n])
    ladder(t_hi, t_lo, v_hi, v_lo, refs[n:])


def chip(o, sign, relative):
    if not relative:
        return o
    x, y, _, _ = here()
    dx, dy = OFFSETS[o]
    return 2 * ((x + 4 + sign * dx) % 4) + (y + dy) % 2


def add_rel_kernel(*refs):
    msgs, previous, out = refs[:8], refs[8], refs[9]
    group = lane_group()
    narrow = [[jnp.zeros((8, LANES), jnp.float32) for _ in range(4)] for _ in range(2)]
    for o in range(8):
        q = chip(o, -1, True)
        for t in range(TILES):
            at = pl.ds(pl.multiple_of((q * TILES + t) * LANES, LANES), LANES)
            out[:, at] = previous[:, at] + msgs[o][t * ROWS : (t + 1) * ROWS, :]
        folded = msgs[o][TILES * ROWS :, :]
        for g in range(4):
            part = pltpu.roll(folded, (ROWS * (q % 4 + 4 - g)) % LANES, 1)
            for j in range(2):
                narrow[j][g] = jnp.where(group + 4 * j == q, part, narrow[j][g])
    for j in range(2):
        at = slice(SPLIT + j * LANES, SPLIT + (j + 1) * LANES)
        out[:, at] = previous[:, at] + jnp.concatenate(narrow[j], axis=0)


def call(kernel, outs, args, flops=0, scratch=(), limit=16):
    moved = sum(a.size * a.dtype.itemsize for a in list(args) + list(outs))
    return pl.pallas_call(
        kernel,
        out_shape=outs,
        in_specs=[pl.BlockSpec(memory_space=pltpu.VMEM)] * len(args),
        out_specs=jax.tree.map(lambda _: pl.BlockSpec(memory_space=pltpu.VMEM), outs),
        scratch_shapes=list(scratch),
        compiler_params=pltpu.CompilerParams(vmem_limit_bytes=limit * MIB),
        cost_estimate=pl.CostEstimate(flops=flops, bytes_accessed=moved, transcendentals=0),
    )(*args)


def f32(*shape):
    return jax.ShapeDtypeStruct(shape, jnp.float32)


GROUPS = ((2,), (1, 3))


def body(amplitudes, integrals, previous):
    msg, stack = f32(MSG, LANES), f32(8, MSG, LANES)
    beside = over_rows(amplitudes, lambda z, y, k: (z, y + 1))
    sent = call(pack_kernel, [stack], [integrals])[0]
    sent, beside = lax.optimization_barrier((sent, beside))
    part = call(tiles_kernel, [f32(16, LANES)], [amplitudes, beside])[0]
    part = call(join_kernel, [f32(32, LANES)], [part, over_rows(part, lambda z, y, k: (z + 4, y))])[0]
    parts = [
        part,
        over_rows(part, lambda z, y, k: (z + 1, y)),
        over_rows(part, lambda z, y, k: (z - 1, y)),
        over_rows(part, lambda z, y, k: (z + 2 - 4 * k, y)),
    ]
    own = call(collect_kernel, [f32(128, LANES)], parts)[0]
    pair = call(join_kernel, [f32(256, LANES)], [own, to_chip(own, 0, 1)])[0]
    mine, _ = lax.optimization_barrier((over_chips(sent), pair))
    other = swap_cores(mine)
    amps = {dx: to_chip(pair, dx, 0) for group in GROUPS for dx in group}
    flops = 3 * 2 * 64 * 512 * 1440
    v_shape = jax.ShapeDtypeStruct((512, 12 * LANES), jnp.bfloat16)
    near, far, *v = call(first_kernel, [msg] * 2 + [v_shape] * 2, [mine, other, pair], flops, limit=32)
    back = {(0, 0): near, (0, 1): to_chip(far, 0, 1)}
    for group in GROUPS:
        n = len(group)
        if group == GROUPS[-1]:
            *v, back[(0, 1)] = lax.optimization_barrier((*v, back[(0, 1)]))
        args = list(v) + [amps[dx] for dx in group]
        out = call(functools.partial(later_kernel, n), [msg] * 2 * n, args, n * flops, limit=32)
        for j, dx in enumerate(group):
            for dy in range(2):
                back[(4 - dx, dy)] = to_chip(out[2 * j + dy], 4 - dx, dy)
    return call(add_rel_kernel, [f32(*previous.shape)], [back[o] for o in OFFSETS] + [previous])[0]


def solution(mesh):
    in_specs = (P(("col", "row"), None), P("col", "row"), P("col", "row"))
    out_specs = P("col", "row")
    return jax.shard_map(body, mesh=mesh, in_specs=in_specs, out_specs=out_specs, check_vma=False)
```

```python
import functools

import jax
import jax.numpy as jnp
from jax import lax
from jax.experimental import pallas as pl
from jax.experimental.pallas import tpu as pltpu
from jax.sharding import PartitionSpec as P

LANES = 128
ROWS = 32
TILES = 11
SPLIT = 8 * TILES * LANES
MSG = TILES * ROWS + 8
MIB = 1 << 20
OVER_CHIPS = [[c for c in range(16) if c % 2 == k] for k in range(2)]
OFFSETS = [(dx, dy) for dx in range(4) for dy in range(2)]


def cols(f):
    pairs = []
    for c in range(16):
        x, y, k = f(c >> 2, (c >> 1) & 1, c & 1)
        pairs.append((c, 4 * (x % 4) + 2 * (y % 2) + k % 2))
    return pairs


def rows(f):
    pairs = []
    for d in range(256):
        r, c = d >> 4, d & 15
        z, y = f(r >> 1, r & 1, c & 1)
        pairs.append((d, 16 * (2 * (z % 8) + y % 2) + c))
    return pairs


def over_chips(a):
    return lax.all_to_all(a, "col", 0, 0, tiled=True, axis_index_groups=OVER_CHIPS)


def to_chip(a, dx, dy):
    return lax.ppermute(a, "col", cols(lambda x, y, k: (x + dx, y + dy, k)))


def swap_cores(a):
    return lax.ppermute(a, "col", cols(lambda x, y, k: (x, y, k + 1)))


def over_rows(a, f):
    return lax.ppermute(a, ("row", "col"), rows(f))


def here():
    col, row = lax.axis_index("col"), lax.axis_index("row")
    return col // 4, (col // 2) % 2, col % 2, row


def split(a):
    hi = a.astype(jnp.bfloat16)
    return hi, (a - hi.astype(jnp.float32)).astype(jnp.bfloat16)


def lane_group():
    return lax.broadcasted_iota(jnp.int32, (8, LANES), 1) // ROWS


def pack_kernel(v, msgs):
    for q in range(8):
        for t in range(TILES):
            at = (q * TILES + t) * LANES
            msgs[q, t * ROWS : (t + 1) * ROWS, :] = v[:, at : at + LANES]
        at = SPLIT + q // 4 * LANES
        folded = v[:8, at : at + LANES]
        for g in range(4):
            part = pltpu.roll(v[8 * g : 8 * g + 8, at : at + LANES], (ROWS * (g + 4 - q % 4)) % LANES, 1)
            folded = jnp.where(lane_group() == g, part, folded)
        msgs[q, TILES * ROWS :, :] = folded


def tiles_kernel(a, b, out):
    for n, part in enumerate((a, b)):
        rows = [part[i : i + 1, c * LANES : (c + 1) * LANES] for i in range(2) for c in range(4)]
        out[8 * n : 8 * n + 8, :] = jnp.concatenate(rows, axis=0)


def join_kernel(a, b, out):
    n = a.shape[0]
    out[:n, :] = a[...]
    out[n:, :] = b[...]


def collect_kernel(*refs):
    parts, out = refs[:4], refs[4]
    _, _, k, row = here()
    for jz, part in enumerate(parts):
        back = (0, 1, 7, 2 + 4 * k)[jz]
        for j4 in range(2):
            for jy in range(2):
                r = 2 * ((row // 2 + 16 - back - 4 * j4) % 8) + (row + jy) % 2
                j = 2 * j4 + jy
                out[pl.ds(pl.multiple_of(8 * r, 8), 8), :] = part[8 * j : 8 * j + 8, :]


def unpack(msg, v_hi, v_lo, at):
    at = pl.ds(pl.multiple_of(at, ROWS), ROWS)
    for t in range(TILES):
        hi, lo = split(msg[t * ROWS : (t + 1) * ROWS, :])
        v_hi[at, t * LANES : (t + 1) * LANES] = hi
        v_lo[at, t * LANES : (t + 1) * LANES] = lo
    folded = msg[TILES * ROWS :, :]
    rows = [folded] + [pltpu.roll(folded, LANES - ROWS * g, 1) for g in range(1, 4)]
    hi, lo = split(jnp.concatenate(rows, axis=0))
    v_hi[at, TILES * LANES :] = hi
    v_lo[at, TILES * LANES :] = lo


def ladder(t_hi, t_lo, v_hi, v_lo, msgs):
    dot = functools.partial(jnp.dot, preferred_element_type=jnp.float32)
    for j in range(6):
        lanes = slice(2 * j * LANES, (2 * j + 2) * LANES)
        hi, lo = v_hi[:, lanes], v_lo[:, lanes]
        out = dot(t_hi, hi) + (dot(t_hi, lo) + dot(t_lo, hi))
        for q, msg in enumerate(msgs):
            rows = out[q * ROWS : (q + 1) * ROWS]
            msg[2 * j * ROWS : (2 * j + 1) * ROWS, :] = rows[:, :LANES]
            if j < 5:
                msg[(2 * j + 1) * ROWS : (2 * j + 2) * ROWS, :] = rows[:, LANES:]
            else:
                folded = rows[:8, LANES:]
                for g in range(1, 4):
                    part = pltpu.roll(rows[8 * g : 8 * g + 8, LANES:], ROWS * g, 1)
                    folded = jnp.where(lane_group() == g, part, folded)
                msg[TILES * ROWS :, :] = folded


def amplitude_rows(amps):
    his, los = [], []
    for amp in amps:
        for h in range(2):
            parts = [split(amp[pl.ds(128 * h + c, ROWS, stride=4), :]) for c in range(4)]
            his.append(jnp.concatenate([p[0] for p in parts], axis=1))
            los.append(jnp.concatenate([p[1] for p in parts], axis=1))
    return jnp.concatenate(his, axis=0), jnp.concatenate(los, axis=0)


def first_kernel(mine, other, amp, *refs):
    msgs, (v_hi, v_lo) = refs[:2], refs[2:4]
    _, _, k, _ = here()
    for q in range(8):
        unpack(mine.at[q], v_hi, v_lo, (2 * q + k) * ROWS)
        unpack(other.at[q], v_hi, v_lo, (2 * q + 1 - k) * ROWS)
    t_hi, t_lo = amplitude_rows([amp])
    ladder(t_hi, t_lo, v_hi, v_lo, msgs)


def later_kernel(n, v_hi, v_lo, *refs):
    t_hi, t_lo = amplitude_rows(refs[:n])
    ladder(t_hi, t_lo, v_hi, v_lo, refs[n:])


def chip(o, sign, relative):
    if not relative:
        return o
    x, y, _, _ = here()
    dx, dy = OFFSETS[o]
    return 2 * ((x + 4 + sign * dx) % 4) + (y + dy) % 2


WIDE = TILES * LANES
EARLY = [0, 1, 4, 5]
LATE = [2, 3, 6, 7]


def narrow_columns(msgs, offsets, start):
    group = lane_group()
    parts = [[start[8 * g : 8 * g + 8, j * LANES : (j + 1) * LANES] for g in range(4)] for j in range(2)]
    for o, msg in zip(offsets, msgs):
        q = chip(o, -1, True)
        folded = msg[TILES * ROWS :, :]
        for g in range(4):
            part = pltpu.roll(folded, (ROWS * (q % 4 + 4 - g)) % LANES, 1)
            for j in range(2):
                parts[j][g] = parts[j][g] + jnp.where(group + 4 * j == q, part, 0.0)
    return [jnp.concatenate(p, axis=0) for p in parts]


def add_early_kernel(*refs):
    msgs, previous, out, narrow = refs[:4], refs[4], refs[5], refs[6]
    for o, msg in zip(EARLY, msgs):
        q = chip(o, -1, True)
        for t in range(TILES):
            at = pl.ds(pl.multiple_of((q * TILES + t) * LANES, LANES), LANES)
            out[:, at] = previous[:, at] + msg[t * ROWS : (t + 1) * ROWS, :]
    for j, value in enumerate(narrow_columns(msgs, EARLY, previous[:, SPLIT:])):
        narrow[:, j * LANES : (j + 1) * LANES] = value


def add_late_kernel(*refs):
    msgs, previous, narrow, _, out, blocks, last, sems = refs[:4], *refs[4:11]
    copies = []
    for n, (o, msg) in enumerate(zip(LATE, msgs)):
        start = chip(o, -1, True) * WIDE
        for t in range(TILES):
            at = pl.ds(pl.multiple_of(start + t * LANES, LANES), LANES)
            blocks[n, :, t * LANES : (t + 1) * LANES] = previous[:, at] + msg[t * ROWS : (t + 1) * ROWS, :]
        at = pl.ds(pl.multiple_of(start, LANES), WIDE)
        copies.append(pltpu.make_async_copy(blocks.at[n], out.at[:, at], sems.at[n]))
        copies[-1].start()
    for j, value in enumerate(narrow_columns(msgs, LATE, narrow[...])):
        last[:, j * LANES : (j + 1) * LANES] = value
    copies.append(pltpu.make_async_copy(last, out.at[:, pl.ds(SPLIT, 2 * LANES)], sems.at[4]))
    copies[-1].start()
    for copy in copies:
        copy.wait()


def call(kernel, outs, args, flops=0, scratch=(), limit=16):
    moved = sum(a.size * a.dtype.itemsize for a in list(args) + list(outs))
    return pl.pallas_call(
        kernel,
        out_shape=outs,
        in_specs=[pl.BlockSpec(memory_space=pltpu.VMEM)] * len(args),
        out_specs=jax.tree.map(lambda _: pl.BlockSpec(memory_space=pltpu.VMEM), outs),
        scratch_shapes=list(scratch),
        compiler_params=pltpu.CompilerParams(vmem_limit_bytes=limit * MIB),
        cost_estimate=pl.CostEstimate(flops=flops, bytes_accessed=moved, transcendentals=0),
    )(*args)


def f32(*shape):
    return jax.ShapeDtypeStruct(shape, jnp.float32)


GROUPS = ((2,), (1, 3))


def body(amplitudes, integrals, previous):
    msg, stack = f32(MSG, LANES), f32(8, MSG, LANES)
    beside = over_rows(amplitudes, lambda z, y, k: (z, y + 1))
    sent = call(pack_kernel, [stack], [integrals])[0]
    sent, beside = lax.optimization_barrier((sent, beside))
    part = call(tiles_kernel, [f32(16, LANES)], [amplitudes, beside])[0]
    part = call(join_kernel, [f32(32, LANES)], [part, over_rows(part, lambda z, y, k: (z + 4, y))])[0]
    parts = [
        part,
        over_rows(part, lambda z, y, k: (z + 1, y)),
        over_rows(part, lambda z, y, k: (z - 1, y)),
        over_rows(part, lambda z, y, k: (z + 2 - 4 * k, y)),
    ]
    own = call(collect_kernel, [f32(128, LANES)], parts)[0]
    pair = call(join_kernel, [f32(256, LANES)], [own, to_chip(own, 0, 1)])[0]
    mine, _ = lax.optimization_barrier((over_chips(sent), pair))
    other = swap_cores(mine)
    amps = {dx: to_chip(pair, dx, 0) for group in GROUPS for dx in group}
    flops = 3 * 2 * 64 * 512 * 1440
    v_shape = jax.ShapeDtypeStruct((512, 12 * LANES), jnp.bfloat16)
    near, far, *v = call(first_kernel, [msg] * 2 + [v_shape] * 2, [mine, other, pair], flops, limit=32)
    back = {(0, 0): near, (0, 1): to_chip(far, 0, 1)}
    for group in GROUPS:
        n = len(group)
        if group == GROUPS[-1]:
            *v, back[(0, 1)] = lax.optimization_barrier((*v, back[(0, 1)]))
        args = list(v) + [amps[dx] for dx in group]
        out = call(functools.partial(later_kernel, n), [msg] * 2 * n, args, n * flops, limit=32)
        for j, dx in enumerate(group):
            for dy in range(2):
                back[(4 - dx, dy)] = to_chip(out[2 * j + dy], 4 - dx, dy)
    whole, narrow = f32(*previous.shape), f32(ROWS, 2 * LANES)
    early = [back[OFFSETS[o]] for o in EARLY] + [previous]
    partial, narrow = call(add_early_kernel, [whole, narrow], early)
    vmem, hbm = pl.BlockSpec(memory_space=pltpu.VMEM), pl.BlockSpec(memory_space=pl.ANY)
    return pl.pallas_call(
        add_late_kernel,
        out_shape=whole,
        in_specs=[vmem] * 6 + [hbm],
        out_specs=hbm,
        input_output_aliases={6: 0},
        scratch_shapes=[
            pltpu.VMEM((4, ROWS, WIDE), jnp.float32),
            pltpu.VMEM((ROWS, 2 * LANES), jnp.float32),
            pltpu.SemaphoreType.DMA((5,)),
        ],
        compiler_params=pltpu.CompilerParams(vmem_limit_bytes=16 * MIB),
        cost_estimate=pl.CostEstimate(flops=0, bytes_accessed=3 * 4 * ROWS * 4 * WIDE, transcendentals=0),
    )(*[back[OFFSETS[o]] for o in LATE], previous, narrow, partial)


def solution(mesh):
    in_specs = (P(("col", "row"), None), P("col", "row"), P("col", "row"))
    out_specs = P("col", "row")
    return jax.shard_map(body, mesh=mesh, in_specs=in_specs, out_specs=out_specs, check_vma=False)
```

```python
import functools

import jax
import jax.numpy as jnp
from jax import lax
from jax.experimental import pallas as pl
from jax.experimental.pallas import tpu as pltpu
from jax.sharding import PartitionSpec as P

LANES = 128
ROWS = 32
TILES = 11
SPLIT = 8 * TILES * LANES
MSG = TILES * ROWS + 8
MIB = 1 << 20
OVER_CHIPS = [[c for c in range(16) if c % 2 == k] for k in range(2)]
OFFSETS = [(dx, dy) for dx in range(4) for dy in range(2)]


def cols(f):
    pairs = []
    for c in range(16):
        x, y, k = f(c >> 2, (c >> 1) & 1, c & 1)
        pairs.append((c, 4 * (x % 4) + 2 * (y % 2) + k % 2))
    return pairs


def rows(f):
    pairs = []
    for d in range(256):
        r, c = d >> 4, d & 15
        z, y = f(r >> 1, r & 1, c & 1)
        pairs.append((d, 16 * (2 * (z % 8) + y % 2) + c))
    return pairs


def over_chips(a):
    return lax.all_to_all(a, "col", 0, 0, tiled=True, axis_index_groups=OVER_CHIPS)


def to_chip(a, dx, dy):
    return lax.ppermute(a, "col", cols(lambda x, y, k: (x + dx, y + dy, k)))


def swap_cores(a):
    return lax.ppermute(a, "col", cols(lambda x, y, k: (x, y, k + 1)))


def over_rows(a, f):
    return lax.ppermute(a, ("row", "col"), rows(f))


def here():
    col, row = lax.axis_index("col"), lax.axis_index("row")
    return col // 4, (col // 2) % 2, col % 2, row


def split(a):
    hi = a.astype(jnp.bfloat16)
    return hi, (a - hi.astype(jnp.float32)).astype(jnp.bfloat16)


def lane_group():
    return lax.broadcasted_iota(jnp.int32, (8, LANES), 1) // ROWS


def pack_kernel(v, msgs):
    for q in range(8):
        for t in range(TILES):
            at = (q * TILES + t) * LANES
            msgs[q, t * ROWS : (t + 1) * ROWS, :] = v[:, at : at + LANES]
        at = SPLIT + q // 4 * LANES
        folded = v[:8, at : at + LANES]
        for g in range(4):
            part = pltpu.roll(v[8 * g : 8 * g + 8, at : at + LANES], (ROWS * (g + 4 - q % 4)) % LANES, 1)
            folded = jnp.where(lane_group() == g, part, folded)
        msgs[q, TILES * ROWS :, :] = folded


def tiles_kernel(a, b, out):
    for n, part in enumerate((a, b)):
        rows = [part[i : i + 1, c * LANES : (c + 1) * LANES] for i in range(2) for c in range(4)]
        out[8 * n : 8 * n + 8, :] = jnp.concatenate(rows, axis=0)


def join_kernel(a, b, out):
    n = a.shape[0]
    out[:n, :] = a[...]
    out[n:, :] = b[...]


def collect_kernel(*refs):
    parts, out = refs[:4], refs[4]
    _, _, k, row = here()
    for jz, part in enumerate(parts):
        back = (0, 1, 7, 2 + 4 * k)[jz]
        for j4 in range(2):
            for jy in range(2):
                r = 2 * ((row // 2 + 16 - back - 4 * j4) % 8) + (row + jy) % 2
                j = 2 * j4 + jy
                out[pl.ds(pl.multiple_of(8 * r, 8), 8), :] = part[8 * j : 8 * j + 8, :]


def unpack(msg, v_hi, v_lo, at):
    at = pl.ds(pl.multiple_of(at, ROWS), ROWS)
    for t in range(TILES):
        hi, lo = split(msg[t * ROWS : (t + 1) * ROWS, :])
        v_hi[at, t * LANES : (t + 1) * LANES] = hi
        v_lo[at, t * LANES : (t + 1) * LANES] = lo
    folded = msg[TILES * ROWS :, :]
    rows = [folded] + [pltpu.roll(folded, LANES - ROWS * g, 1) for g in range(1, 4)]
    hi, lo = split(jnp.concatenate(rows, axis=0))
    v_hi[at, TILES * LANES :] = hi
    v_lo[at, TILES * LANES :] = lo


def ladder(t_hi, t_lo, v_hi, v_lo, msgs):
    dot = functools.partial(jnp.dot, preferred_element_type=jnp.float32)
    for j in range(6):
        lanes = slice(2 * j * LANES, (2 * j + 2) * LANES)
        hi, lo = v_hi[:, lanes], v_lo[:, lanes]
        out = dot(t_hi, hi) + (dot(t_hi, lo) + dot(t_lo, hi))
        for q, msg in enumerate(msgs):
            rows = out[q * ROWS : (q + 1) * ROWS]
            msg[2 * j * ROWS : (2 * j + 1) * ROWS, :] = rows[:, :LANES]
            if j < 5:
                msg[(2 * j + 1) * ROWS : (2 * j + 2) * ROWS, :] = rows[:, LANES:]
            else:
                folded = rows[:8, LANES:]
                for g in range(1, 4):
                    part = pltpu.roll(rows[8 * g : 8 * g + 8, LANES:], ROWS * g, 1)
                    folded = jnp.where(lane_group() == g, part, folded)
                msg[TILES * ROWS :, :] = folded


def amplitude_rows(amps):
    his, los = [], []
    for amp in amps:
        for h in range(2):
            parts = [split(amp[pl.ds(128 * h + c, ROWS, stride=4), :]) for c in range(4)]
            his.append(jnp.concatenate([p[0] for p in parts], axis=1))
            los.append(jnp.concatenate([p[1] for p in parts], axis=1))
    return jnp.concatenate(his, axis=0), jnp.concatenate(los, axis=0)


def first_kernel(mine, other, amp, *refs):
    msgs, (v_hi, v_lo) = refs[:2], refs[2:4]
    _, _, k, _ = here()
    for q in range(8):
        unpack(mine.at[q], v_hi, v_lo, (2 * q + k) * ROWS)
        unpack(other.at[q], v_hi, v_lo, (2 * q + 1 - k) * ROWS)
    t_hi, t_lo = amplitude_rows([amp])
    ladder(t_hi, t_lo, v_hi, v_lo, msgs)


def later_kernel(n, v_hi, v_lo, *refs):
    t_hi, t_lo = amplitude_rows(refs[:n])
    ladder(t_hi, t_lo, v_hi, v_lo, refs[n:])


def chip(o, sign, relative):
    if not relative:
        return o
    x, y, _, _ = here()
    dx, dy = OFFSETS[o]
    return 2 * ((x + 4 + sign * dx) % 4) + (y + dy) % 2


WIDE = TILES * LANES
EARLY = [0, 1, 4, 5]
LATE = [2, 3, 6, 7]


def narrow_columns(msgs, offsets, start):
    group = lane_group()
    parts = [[start[8 * g : 8 * g + 8, j * LANES : (j + 1) * LANES] for g in range(4)] for j in range(2)]
    for o, msg in zip(offsets, msgs):
        q = chip(o, -1, True)
        folded = msg[TILES * ROWS :, :]
        for g in range(4):
            part = pltpu.roll(folded, (ROWS * (q % 4 + 4 - g)) % LANES, 1)
            for j in range(2):
                parts[j][g] = parts[j][g] + jnp.where(group + 4 * j == q, part, 0.0)
    return [jnp.concatenate(p, axis=0) for p in parts]


def add_early_kernel(*refs):
    msgs, previous, out, narrow = refs[:4], refs[4], refs[5], refs[6]
    for o, msg in zip(EARLY, msgs):
        q = chip(o, -1, True)
        for t in range(TILES):
            at = pl.ds(pl.multiple_of((q * TILES + t) * LANES, LANES), LANES)
            out[:, at] = previous[:, at] + msg[t * ROWS : (t + 1) * ROWS, :]
    for j, value in enumerate(narrow_columns(msgs, EARLY, previous[:, SPLIT:])):
        narrow[:, j * LANES : (j + 1) * LANES] = value


def write_blocks(offsets, msgs, previous, out, blocks, sems):
    copies = []
    for n, (o, msg) in enumerate(zip(offsets, msgs)):
        start = chip(o, -1, True) * WIDE
        for t in range(TILES):
            at = pl.ds(pl.multiple_of(start + t * LANES, LANES), LANES)
            blocks[n, :, t * LANES : (t + 1) * LANES] = previous[:, at] + msg[t * ROWS : (t + 1) * ROWS, :]
        at = pl.ds(pl.multiple_of(start, LANES), WIDE)
        copies.append(pltpu.make_async_copy(blocks.at[n], out.at[:, at], sems.at[n]))
        copies[-1].start()
    return copies


def add_middle_kernel(m0, m1, previous, _, out, blocks, sems):
    for copy in write_blocks(LATE[:2], (m0, m1), previous, out, blocks, sems):
        copy.wait()


def add_late_kernel(*refs):
    msgs, previous, narrow, _, out, blocks, last, sems = refs[:4], *refs[4:11]
    copies = write_blocks(LATE[2:], msgs[2:], previous, out, blocks, sems)
    for j, value in enumerate(narrow_columns(msgs, LATE, narrow[...])):
        last[:, j * LANES : (j + 1) * LANES] = value
    copies.append(pltpu.make_async_copy(last, out.at[:, pl.ds(SPLIT, 2 * LANES)], sems.at[2]))
    copies[-1].start()
    for copy in copies:
        copy.wait()


def add_in_place(kernel, args, scratch, sems):
    vmem, hbm = pl.BlockSpec(memory_space=pltpu.VMEM), pl.BlockSpec(memory_space=pl.ANY)
    n = len(args) - 1
    return pl.pallas_call(
        kernel,
        out_shape=f32(*args[n].shape),
        in_specs=[vmem] * n + [hbm],
        out_specs=hbm,
        input_output_aliases={n: 0},
        scratch_shapes=[pltpu.VMEM((2, ROWS, WIDE), jnp.float32)] + scratch + [pltpu.SemaphoreType.DMA((sems,))],
        compiler_params=pltpu.CompilerParams(vmem_limit_bytes=16 * MIB),
        cost_estimate=pl.CostEstimate(flops=0, bytes_accessed=3 * 2 * ROWS * 4 * WIDE, transcendentals=0),
    )(*args)


def call(kernel, outs, args, flops=0, scratch=(), limit=16):
    moved = sum(a.size * a.dtype.itemsize for a in list(args) + list(outs))
    return pl.pallas_call(
        kernel,
        out_shape=outs,
        in_specs=[pl.BlockSpec(memory_space=pltpu.VMEM)] * len(args),
        out_specs=jax.tree.map(lambda _: pl.BlockSpec(memory_space=pltpu.VMEM), outs),
        scratch_shapes=list(scratch),
        compiler_params=pltpu.CompilerParams(vmem_limit_bytes=limit * MIB),
        cost_estimate=pl.CostEstimate(flops=flops, bytes_accessed=moved, transcendentals=0),
    )(*args)


def f32(*shape):
    return jax.ShapeDtypeStruct(shape, jnp.float32)


GROUPS = ((2,), (1, 3))


def body(amplitudes, integrals, previous):
    msg, stack = f32(MSG, LANES), f32(8, MSG, LANES)
    beside = over_rows(amplitudes, lambda z, y, k: (z, y + 1))
    sent = call(pack_kernel, [stack], [integrals])[0]
    sent, beside = lax.optimization_barrier((sent, beside))
    part = call(tiles_kernel, [f32(16, LANES)], [amplitudes, beside])[0]
    part = call(join_kernel, [f32(32, LANES)], [part, over_rows(part, lambda z, y, k: (z + 4, y))])[0]
    parts = [
        part,
        over_rows(part, lambda z, y, k: (z + 1, y)),
        over_rows(part, lambda z, y, k: (z - 1, y)),
        over_rows(part, lambda z, y, k: (z + 2 - 4 * k, y)),
    ]
    own = call(collect_kernel, [f32(128, LANES)], parts)[0]
    pair = call(join_kernel, [f32(256, LANES)], [own, to_chip(own, 0, 1)])[0]
    mine, _ = lax.optimization_barrier((over_chips(sent), pair))
    other = swap_cores(mine)
    amps = {dx: to_chip(pair, dx, 0) for group in GROUPS for dx in group}
    flops = 3 * 2 * 64 * 512 * 1440
    v_shape = jax.ShapeDtypeStruct((512, 12 * LANES), jnp.bfloat16)
    near, far, *v = call(first_kernel, [msg] * 2 + [v_shape] * 2, [mine, other, pair], flops, limit=32)
    back = {(0, 0): near, (0, 1): to_chip(far, 0, 1)}
    for group in GROUPS:
        n = len(group)
        if group == GROUPS[-1]:
            *v, back[(0, 1)] = lax.optimization_barrier((*v, back[(0, 1)]))
        args = list(v) + [amps[dx] for dx in group]
        out = call(functools.partial(later_kernel, n), [msg] * 2 * n, args, n * flops, limit=32)
        for j, dx in enumerate(group):
            for dy in range(2):
                back[(4 - dx, dy)] = to_chip(out[2 * j + dy], 4 - dx, dy)
    whole, narrow = f32(*previous.shape), f32(ROWS, 2 * LANES)
    early = [back[OFFSETS[o]] for o in EARLY] + [previous]
    partial, narrow = call(add_early_kernel, [whole, narrow], early)
    late = [back[OFFSETS[o]] for o in LATE]
    partial = add_in_place(add_middle_kernel, late[:2] + [previous, partial], [], 2)
    last = pltpu.VMEM((ROWS, 2 * LANES), jnp.float32)
    return add_in_place(add_late_kernel, late + [previous, narrow, partial], [last], 3)


def solution(mesh):
    in_specs = (P(("col", "row"), None), P("col", "row"), P("col", "row"))
    out_specs = P("col", "row")
    return jax.shard_map(body, mesh=mesh, in_specs=in_specs, out_specs=out_specs, check_vma=False)
```
